512 devices in a mesh: row: 16 (over y, z_lo), col: 32 (over z_hi, x, core).
Axes of the slice: x: 4, y: 4, z: 16 (z_hi: 4, z_lo: 4; z = z_hi * 4 + z_lo), core: 2. Of those that a mesh axis runs over, the one named last changes fastest.
Arguments:
- grid: bfloat16 [512, 1024, 256], P('row', 'col'), may hold values from -6 to 6
- row_gain: float32 [256], replicated, may hold values from 0.1 to 1.9
- row_qkv: bfloat16 [256, 768], replicated, may hold values from -24 to 24, as said below
- row_out: bfloat16 [256, 256], replicated, may hold values from -1.5 to 1.5
- col_gain: float32 [256], replicated, may hold values from 0.1 to 1.9
- col_qkv: bfloat16 [256, 768], replicated, may hold values from -24 to 24, as said below
- col_out: bfloat16 [256, 256], replicated, may hold values from -1.5 to 1.5
Outputs:
- updated: bfloat16 [512, 1024, 256], P('row', 'col')
The draws below stay inside these ranges and needn't reach their ends.
Inputs may be any that keep to these rules, and one draw needn't show every extreme that they name: `row_qkv`: projection weights of fan-in 256. `col_qkv`: projection weights of fan-in 256.
All inputs are finite; a program needn't handle non-finite values.
Results may differ from the reference program's by a relative error of at most 0.028.
Values may be sent and summed in bfloat16 or wider, within the bound.
No kernel may reach another device: no remote copies, remote signals or barrier semaphores. Data moves between devices by JAX's collectives and lax.ppermute only.
A program may use at most 64 MiB of HBM per device.

```python
import jax
import jax.numpy as jnp
from jax import lax

C = 256
HEADS = 8
H = 512
W = 1024


def qkv_weights(key):
    base = jax.random.normal(key, (C, 3 * C), jnp.float32) * C ** (-0.5)
    return jnp.clip(base, -24.0, 24.0).astype(jnp.bfloat16)


def draw_row_qkv(key, part):
    key = jax.random.fold_in(key, 11)
    return qkv_weights(key)


def draw_col_qkv(key, part):
    key = jax.random.fold_in(key, 12)
    return qkv_weights(key)


def steps_of(own_key, shape, split, least, high):
    level = 1.0
    for position, shards_of in split:
        draws = jax.random.uniform(jax.random.fold_in(jax.random.fold_in(own_key, 6), position), (shards_of,), jnp.float32, least / len(split), high / len(split))
        level = level * jnp.repeat(jnp.exp(draws), shape[position] // shards_of).reshape((-1,) + (1,) * (len(shape) - 1 - position))
    return level


def gaussian(own_key, dims, scale, reach, cuts=(), dtype=jnp.bfloat16):
    loudness = steps_of(own_key, dims, cuts, -0.22, 0.18) if cuts else 1.0
    drawn = jax.random.normal(own_key, dims, jnp.float32) * scale * loudness
    return jnp.minimum(jnp.maximum(drawn, -reach), reach).astype(dtype)


def setup_inputs(seed: int = 0) -> dict:
    arg_keys = jax.random.split(jax.random.key(seed), 8)
    grid = gaussian(arg_keys[0], (H, W, C), 1.0, 6.0, ((0, 16), (1, 32)))
    row_gain = jnp.clip(1.0 + 0.18 * jax.random.normal(arg_keys[1], (C,), jnp.float32), 0.1, 1.9)
    row_qkv = draw_row_qkv(jax.random.fold_in(arg_keys[7], 71), 0)
    row_out = gaussian(arg_keys[3], (C, C), (C // 16) ** -0.5, 1.5)
    col_gain = jnp.clip(1.0 + 0.18 * jax.random.normal(arg_keys[4], (C,), jnp.float32), 0.1, 1.9)
    col_qkv = draw_col_qkv(jax.random.fold_in(arg_keys[7], 71), 0)
    col_out = gaussian(arg_keys[6], (C, C), (C // 16) ** -0.5, 1.5)
    return dict(grid=grid, row_gain=row_gain, row_qkv=row_qkv, row_out=row_out, col_gain=col_gain, col_qkv=col_qkv, col_out=col_out)


def layer_norm(values, gain):
    as_float = values.astype(jnp.float32)
    mean_val = lax.optimization_barrier(jnp.mean(as_float, axis=-1, keepdims=True))
    centred = as_float - mean_val
    variance = lax.optimization_barrier(jnp.mean(centred * centred, axis=-1, keepdims=True))
    return (centred * lax.rsqrt(variance + 1e-05) * gain.astype(jnp.float32)).astype(jnp.bfloat16)

def heads_attend(packed):
    lines_count, length, triple = packed.shape
    channels = triple // 3
    head_dim = channels // HEADS
    stacked = packed.reshape(lines_count, length, 3, HEADS, head_dim).transpose(2, 3, 0, 1, 4)

    def single_head(triplet):
        queries, keys, values = triplet
        scores = jnp.einsum('nld,nmd->nlm', queries.astype(jnp.float32), keys.astype(jnp.float32)) * head_dim ** (-0.5)
        peak = lax.optimization_barrier(jnp.max(scores, axis=-1, keepdims=True))
        exponent = jnp.exp(scores - peak)
        shares = (exponent / lax.optimization_barrier(jnp.sum(exponent, axis=-1, keepdims=True))).astype(jnp.bfloat16)
        return jnp.einsum('nlm,nmd->nld', shares.astype(jnp.float32), values.astype(jnp.float32))
    per_head = lax.map(single_head, (stacked[0], stacked[1], stacked[2]))
    return per_head.transpose(1, 2, 0, 3).reshape(lines_count, length, channels).astype(jnp.bfloat16)

def attend_lines(lines, weight_qkv):

    def grid_line(line):
        packed = jnp.dot(line, weight_qkv, preferred_element_type=jnp.float32).astype(jnp.bfloat16)
        return heads_attend(packed[None])[0]
    return lax.map(grid_line, lines)

def reference(grid, row_gain, row_qkv, row_out, col_gain, col_qkv, col_out):
    rows_all, cols_all, channels = grid.shape
    normed = layer_norm(grid, row_gain)
    attended = attend_lines(normed, row_qkv)
    projected = jnp.dot(attended.reshape(-1, channels), row_out, preferred_element_type=jnp.float32)
    middle = (grid.astype(jnp.float32) + projected.reshape(rows_all, cols_all, channels)).astype(jnp.bfloat16)
    normed_col = layer_norm(middle, col_gain).transpose(1, 0, 2)
    attended_col = attend_lines(normed_col, col_qkv).transpose(1, 0, 2)
    projected_col = jnp.dot(attended_col.reshape(-1, channels), col_out, preferred_element_type=jnp.float32)
    return (middle.astype(jnp.float32) + projected_col.reshape(rows_all, cols_all, channels)).astype(jnp.bfloat16)
```

```python
import functools
import math

import jax
import jax.numpy as jnp
from jax import lax
from jax.experimental import pallas as pl
from jax.experimental.pallas import tpu as pltpu
from jax.sharding import PartitionSpec as P

HEADS = 8
QUERY_BLOCK = 256
EPS = 1e-05


def contract(a, b, dim_a, dim_b):
    dims = (((dim_a,), (dim_b,)), ((), ()))
    return lax.dot_general(a, b, dims, preferred_element_type=jnp.float32)


def layer_norm(values, gain):
    centred = values - jnp.mean(values, axis=-1, keepdims=True)
    variance = jnp.mean(centred * centred, axis=-1, keepdims=True)
    return (centred * lax.rsqrt(variance + EPS) * gain).astype(jnp.bfloat16)


def lines_kernel(cells_ref, gain_ref, qkv_ref, out_ref, result_ref, q_ref, kt_ref, v_ref, att_ref, *, lines):
    cells, width = cells_ref.shape
    length = cells // lines
    head_dim = width // HEADS
    scale = head_dim**-0.5 * math.log2(math.e)
    normed = layer_norm(cells_ref[...].astype(jnp.float32), gain_ref[...])
    q_ref[...] = (contract(normed, qkv_ref[:, :width], 1, 0) * scale).astype(jnp.bfloat16)
    kt_ref[...] = contract(qkv_ref[:, width : 2 * width], normed, 0, 1).astype(jnp.bfloat16)
    v_ref[...] = contract(normed, qkv_ref[:, 2 * width :], 1, 0).astype(jnp.bfloat16)
    block = min(QUERY_BLOCK, length)
    head_of_v = lax.broadcasted_iota(jnp.int32, (length, width), 1) // head_dim
    head_of_q = lax.broadcasted_iota(jnp.int32, (block, width), 1) // head_dim
    zero, one = jnp.zeros((), jnp.bfloat16), jnp.ones((), jnp.bfloat16)
    for line in range(lines):
        keys = slice(line * length, (line + 1) * length)
        for start in range(line * length, (line + 1) * length, block):
            rows = slice(start, start + block)
            attended = jnp.zeros((block, width), jnp.float32)
            for head in range(HEADS):
                queries = jnp.where(head_of_q == head, q_ref[rows, :], zero)
                scores = contract(queries, kt_ref[:, keys], 1, 0)
                peak = jnp.max(scores, axis=1, keepdims=True)
                shares = jnp.exp2(scores - peak).astype(jnp.bfloat16)
                values = jnp.where(head_of_v == head, v_ref[keys, :], one)
                total = contract(shares, values, 1, 0)
                half = width // 2
                sums = jnp.concatenate([total[:, half:], total[:, :half]], axis=1)
                attended = jnp.where(head_of_q == head, total / sums, attended)
            att_ref[rows, :] = attended.astype(jnp.bfloat16)
    added = contract(att_ref[...], out_ref[...], 1, 0)
    result_ref[...] = (cells_ref[...].astype(jnp.float32) + added).astype(jnp.bfloat16)


def attend(cells, gain, qkv, out, lines):
    count, width = cells.shape
    whole = pl.BlockSpec(memory_space=pltpu.VMEM)
    return pl.pallas_call(
        functools.partial(lines_kernel, lines=lines),
        out_shape=jax.ShapeDtypeStruct((count, width), jnp.bfloat16),
        in_specs=[whole] * 4,
        out_specs=whole,
        scratch_shapes=[
            pltpu.VMEM((count, width), jnp.bfloat16),
            pltpu.VMEM((width, count), jnp.bfloat16),
            pltpu.VMEM((count, width), jnp.bfloat16),
            pltpu.VMEM((count, width), jnp.bfloat16),
        ],
        compiler_params=pltpu.CompilerParams(vmem_limit_bytes=40 << 20),
        name=f"attend_{lines}_lines",
    )(cells, gain.reshape(1, width), qkv, out)


def on_device(grid, row_gain, row_qkv, row_out, col_gain, col_qkv, col_out):
    rows_blk, cols_blk, width = grid.shape
    col_count = lax.axis_size("col")
    row_count = lax.axis_size("row")
    pair = cols_blk // row_count
    cells = lax.all_to_all(grid, "col", split_axis=0, concat_axis=0, tiled=True)
    middle = attend(cells.reshape(-1, width), row_gain, row_qkv, row_out, 1)
    to_cols = middle.reshape(col_count, pair, row_count, width).transpose(0, 2, 1, 3)
    to_cols = to_cols.reshape(col_count * row_count, pair, width)
    col_cells = lax.all_to_all(to_cols, ("col", "row"), split_axis=0, concat_axis=0, tiled=True)
    lines = col_cells.transpose(1, 0, 2).reshape(-1, width)
    updated = attend(lines, col_gain, col_qkv, col_out, pair)
    back = updated.reshape(pair, col_count, row_count, width).transpose(2, 1, 0, 3)
    home = lax.all_to_all(back, "row", split_axis=0, concat_axis=0, tiled=True)
    return home.transpose(1, 2, 0, 3).reshape(rows_blk, cols_blk, width)


def solution(mesh):
    in_specs = (P("row", "col", None), P(), P(), P(), P(), P(), P())
    out_specs = P("row", "col", None)
    return jax.shard_map(
        on_device, mesh=mesh, in_specs=in_specs, out_specs=out_specs, check_vma=False
    )
```

```python
import functools
import math

import jax
import jax.numpy as jnp
from jax import lax
from jax.experimental import pallas as pl
from jax.experimental.pallas import tpu as pltpu
from jax.sharding import Mesh
from jax.sharding import PartitionSpec as P

HEADS = 8
Z_LO = 4
QUERY_BLOCK = 256
EPS = 1e-05
ROW = ("z_lo", "y")


def contract(a, b, dim_a, dim_b):
    dims = (((dim_a,), (dim_b,)), ((), ()))
    return lax.dot_general(a, b, dims, preferred_element_type=jnp.float32)


def layer_norm(values, gain):
    centred = values - jnp.mean(values, axis=-1, keepdims=True)
    variance = jnp.mean(centred * centred, axis=-1, keepdims=True)
    return (centred * lax.rsqrt(variance + EPS) * gain).astype(jnp.bfloat16)


def lines_kernel(*refs, lines, passed):
    (cells_ref, gain_ref, qkv_ref, out_ref), refs = refs[:4], refs[4:]
    sources, result_ref, targets = refs[:passed], refs[passed], refs[passed + 1 : 2 * passed + 1]
    q_ref, kt_ref, v_ref, att_ref, *sems = refs[2 * passed + 1 :]
    copies = [pltpu.make_async_copy(s, t, sems[0].at[n]) for n, (s, t) in enumerate(zip(sources, targets))]
    for copy in copies:
        copy.start()
    attend_lines(cells_ref, gain_ref, qkv_ref, out_ref, result_ref, q_ref, kt_ref, v_ref, att_ref, lines)
    for copy in copies:
        copy.wait()


def attend_lines(cells_ref, gain_ref, qkv_ref, out_ref, result_ref, q_ref, kt_ref, v_ref, att_ref, lines):
    cells, width = cells_ref.shape
    length = cells // lines
    head_dim = width // HEADS
    scale = head_dim**-0.5 * math.log2(math.e)
    normed = layer_norm(cells_ref[...].astype(jnp.float32), gain_ref[...])
    q_ref[...] = (contract(normed, qkv_ref[:, :width], 1, 0) * scale).astype(jnp.bfloat16)
    kt_ref[...] = contract(qkv_ref[:, width : 2 * width], normed, 0, 1).astype(jnp.bfloat16)
    v_ref[...] = contract(normed, qkv_ref[:, 2 * width :], 1, 0).astype(jnp.bfloat16)
    block = min(QUERY_BLOCK, length)
    head_of_v = lax.broadcasted_iota(jnp.int32, (length, width), 1) // head_dim
    head_of_q = lax.broadcasted_iota(jnp.int32, (block, width), 1) // head_dim
    zero, one = jnp.zeros((), jnp.bfloat16), jnp.ones((), jnp.bfloat16)
    for line in range(lines):
        keys = slice(line * length, (line + 1) * length)
        for start in range(line * length, (line + 1) * length, block):
            rows = slice(start, start + block)
            attended = jnp.zeros((block, width), jnp.float32)
            for head in range(HEADS):
                queries = jnp.where(head_of_q == head, q_ref[rows, :], zero)
                scores = contract(queries, kt_ref[:, keys], 1, 0)
                peak = jnp.max(scores, axis=1, keepdims=True)
                shares = jnp.exp2(scores - peak).astype(jnp.bfloat16)
                values = jnp.where(head_of_v == head, v_ref[keys, :], one)
                total = contract(shares, values, 1, 0)
                half = width // 2
                sums = jnp.concatenate([total[:, half:], total[:, :half]], axis=1)
                attended = jnp.where(head_of_q == head, total / sums, attended)
            att_ref[rows, :] = attended.astype(jnp.bfloat16)
    added = contract(att_ref[...], out_ref[...], 1, 0)
    result_ref[...] = (cells_ref[...].astype(jnp.float32) + added).astype(jnp.bfloat16)


def attend(cells, gain, qkv, out, lines, passed=()):
    count, width = cells.shape
    whole, anywhere = pl.BlockSpec(memory_space=pltpu.VMEM), pl.BlockSpec(memory_space=pl.ANY)
    results = pl.pallas_call(
        functools.partial(lines_kernel, lines=lines, passed=len(passed)),
        out_shape=[jax.ShapeDtypeStruct(a.shape, a.dtype) for a in (cells, *passed)],
        in_specs=[whole] * 4 + [anywhere] * len(passed),
        out_specs=[whole] * (1 + len(passed)),
        scratch_shapes=[
            pltpu.VMEM((count, width), jnp.bfloat16),
            pltpu.VMEM((width, count), jnp.bfloat16),
            pltpu.VMEM((count, width), jnp.bfloat16),
            pltpu.VMEM((count, width), jnp.bfloat16),
        ]
        + ([pltpu.SemaphoreType.DMA((len(passed),))] if passed else []),
        compiler_params=pltpu.CompilerParams(vmem_limit_bytes=40 << 20),
        name=f"attend_{lines}_lines",
    )(cells, gain, qkv, out, *passed)
    return results if passed else results[0]


def on_device(grid, row_gain, row_qkv, row_out, col_gain, col_qkv, col_out):
    rows_blk, cols_blk, width = grid.shape
    col_count = lax.axis_size("col")
    row_count = lax.axis_size(ROW)
    pair = cols_blk // row_count
    cells = lax.all_to_all(grid, "col", split_axis=0, concat_axis=0, tiled=True)
    col_weights = (col_gain.reshape(1, width), col_qkv, col_out)
    middle, *col_weights = attend(
        cells.reshape(-1, width), row_gain.reshape(1, width), row_qkv, row_out, 1, col_weights
    )
    to_cols = middle.reshape(col_count * row_count, pair, width)
    col_cells = lax.all_to_all(to_cols, ("col", *ROW), split_axis=0, concat_axis=0, tiled=True)
    lines = col_cells.transpose(1, 0, 2).reshape(-1, width)
    updated = attend(lines, *col_weights, pair)
    back = updated.reshape(pair, col_count, row_count, width).transpose(2, 1, 0, 3)
    home = lax.all_to_all(back, ROW, split_axis=0, concat_axis=0, tiled=True)
    return home.transpose(1, 0, 2, 3).reshape(rows_blk, cols_blk, width)


def solution(mesh):
    row_count, col_count = mesh.devices.shape
    split = Mesh(mesh.devices.reshape(row_count // Z_LO, Z_LO, col_count), ("y", "z_lo", "col"))
    in_specs = (P(("y", "z_lo"), "col", None), P(), P(), P(), P(), P(), P())
    out_specs = P(("y", "z_lo"), "col", None)
    return jax.shard_map(
        on_device, mesh=split, in_specs=in_specs, out_specs=out_specs, check_vma=False
    )
```

```python
import functools
import math

import jax
import jax.numpy as jnp
from jax import lax
from jax.experimental import pallas as pl
from jax.experimental.pallas import tpu as pltpu
from jax.sharding import Mesh
from jax.sharding import PartitionSpec as P

HEADS = 8
Z_LO = 4
QUERY_BLOCK = 256
EPS = 1e-05
ROW_CHUNK = 16
ROW = ("z_lo", "y")


def contract(a, b, dim_a, dim_b):
    dims = (((dim_a,), (dim_b,)), ((), ()))
    return lax.dot_general(a, b, dims, preferred_element_type=jnp.float32)


def layer_norm(values, gain):
    centred = values - jnp.mean(values, axis=-1, keepdims=True)
    variance = jnp.mean(centred * centred, axis=-1, keepdims=True)
    return (centred * lax.rsqrt(variance + EPS) * gain).astype(jnp.bfloat16)


def lines_kernel(*refs, lines, passed):
    (cells_ref, gain_ref, qkv_ref, out_ref), refs = refs[:4], refs[4:]
    sources, result_ref, targets = refs[:passed], refs[passed], refs[passed + 1 : 2 * passed + 1]
    q_ref, kt_ref, v_ref, att_ref, *sems = refs[2 * passed + 1 :]
    copies = [pltpu.make_async_copy(s, t, sems[0].at[n]) for n, (s, t) in enumerate(zip(sources, targets))]
    attend_lines(cells_ref, gain_ref, qkv_ref, out_ref, result_ref, q_ref, kt_ref, v_ref, att_ref, lines, copies)
    for copy in copies:
        copy.wait()


def attend_lines(cells_ref, gain_ref, qkv_ref, out_ref, result_ref, q_ref, kt_ref, v_ref, att_ref, lines, copies):
    cells, width = cells_ref.shape
    length = cells // lines
    head_dim = width // HEADS
    scale = head_dim**-0.5 * math.log2(math.e)
    normed = layer_norm(cells_ref[...].astype(jnp.float32), gain_ref[...])
    q_ref[...] = (contract(normed, qkv_ref[:, :width], 1, 0) * scale).astype(jnp.bfloat16)
    kt_ref[...] = contract(qkv_ref[:, width : 2 * width], normed, 0, 1).astype(jnp.bfloat16)
    v_ref[...] = contract(normed, qkv_ref[:, 2 * width :], 1, 0).astype(jnp.bfloat16)
    for copy in copies:
        copy.start()
    block = min(QUERY_BLOCK, length)
    head_of_v = lax.broadcasted_iota(jnp.int32, (length, width), 1) // head_dim
    head_of_q = lax.broadcasted_iota(jnp.int32, (block, width), 1) // head_dim
    zero, one = jnp.zeros((), jnp.bfloat16), jnp.ones((), jnp.bfloat16)
    for line in range(lines):
        keys = slice(line * length, (line + 1) * length)
        for start in range(line * length, (line + 1) * length, block):
            rows = slice(start, start + block)
            attended = jnp.zeros((block, width), jnp.float32)
            for head in range(HEADS):
                queries = jnp.where(head_of_q == head, q_ref[rows, :], zero)
                scores = contract(queries, kt_ref[:, keys], 1, 0)
                peak = jnp.max(scores, axis=1, keepdims=True)
                shares = jnp.exp2(scores - peak).astype(jnp.bfloat16)
                values = jnp.where(head_of_v == head, v_ref[keys, :], one)
                total = contract(shares, values, 1, 0)
                half = width // 2
                sums = jnp.concatenate([total[:, half:], total[:, :half]], axis=1)
                attended = jnp.where(head_of_q == head, total / sums, attended)
            att_ref[rows, :] = attended.astype(jnp.bfloat16)
    added = contract(att_ref[...], out_ref[...], 1, 0)
    result_ref[...] = (cells_ref[...].astype(jnp.float32) + added).astype(jnp.bfloat16)


def attend(cells, gain, qkv, out, lines, passed=()):
    count, width = cells.shape
    whole, anywhere = pl.BlockSpec(memory_space=pltpu.VMEM), pl.BlockSpec(memory_space=pl.ANY)
    results = pl.pallas_call(
        functools.partial(lines_kernel, lines=lines, passed=len(passed)),
        out_shape=[jax.ShapeDtypeStruct(a.shape, a.dtype) for a in (cells, *passed)],
        in_specs=[whole] * 4 + [anywhere] * len(passed),
        out_specs=[whole] * (1 + len(passed)),
        scratch_shapes=[
            pltpu.VMEM((count, width), jnp.bfloat16),
            pltpu.VMEM((width, count), jnp.bfloat16),
            pltpu.VMEM((count, width), jnp.bfloat16),
            pltpu.VMEM((count, width), jnp.bfloat16),
        ]
        + ([pltpu.SemaphoreType.DMA((len(passed),))] if passed else []),
        compiler_params=pltpu.CompilerParams(vmem_limit_bytes=40 << 20),
        name=f"attend_{lines}_lines",
    )(cells, gain, qkv, out, *passed)
    return results if passed else results[0]


def interleave_kernel(home_ref, grid_ref):
    places, pair, _, width = home_ref.shape
    rows = grid_ref.shape[0]
    start = pl.multiple_of(pl.program_id(0) * rows, rows)
    lines = home_ref[:, :, pl.ds(start, rows), :].reshape(places * pair, rows, width)
    grid_ref[...] = jnp.swapaxes(lines, 0, 1)


def interleave(home):
    places, pair, rows, width = home.shape
    return pl.pallas_call(
        interleave_kernel,
        out_shape=jax.ShapeDtypeStruct((rows, places * pair, width), home.dtype),
        grid=(rows // ROW_CHUNK,),
        in_specs=[pl.BlockSpec(memory_space=pltpu.VMEM)],
        out_specs=pl.BlockSpec((ROW_CHUNK, places * pair, width), lambda chunk: (chunk, 0, 0)),
        compiler_params=pltpu.CompilerParams(vmem_limit_bytes=16 << 20),
        name="interleave_columns",
    )(home)


def on_device(grid, row_gain, row_qkv, row_out, col_gain, col_qkv, col_out):
    rows_blk, cols_blk, width = grid.shape
    col_count = lax.axis_size("col")
    row_count = lax.axis_size(ROW)
    pair = cols_blk // row_count
    cells = lax.all_to_all(grid, "col", split_axis=0, concat_axis=0, tiled=True)
    col_weights = (col_gain.reshape(1, width), col_qkv, col_out)
    middle, *col_weights = attend(
        cells.reshape(-1, width), row_gain.reshape(1, width), row_qkv, row_out, 1, col_weights
    )
    to_cols = middle.reshape(col_count * row_count, pair, width)
    col_cells = lax.all_to_all(to_cols, ("col", *ROW), split_axis=0, concat_axis=0, tiled=True)
    lines = col_cells.transpose(1, 0, 2).reshape(-1, width)
    updated = attend(lines, *col_weights, pair)
    back = updated.reshape(pair, col_count, row_count, width).transpose(2, 0, 1, 3)
    home = lax.all_to_all(back, ROW, split_axis=0, concat_axis=0, tiled=True)
    return interleave(home)


def solution(mesh):
    row_count, col_count = mesh.devices.shape
    split = Mesh(mesh.devices.reshape(row_count // Z_LO, Z_LO, col_count), ("y", "z_lo", "col"))
    in_specs = (P(("y", "z_lo"), "col", None), P(), P(), P(), P(), P(), P())
    out_specs = P(("y", "z_lo"), "col", None)
    return jax.shard_map(
        on_device, mesh=split, in_specs=in_specs, out_specs=out_specs, check_vma=False
    )
```

```python
import functools
import math

import jax
import jax.numpy as jnp
from jax import lax
from jax.experimental import pallas as pl
from jax.experimental.pallas import tpu as pltpu
from jax.sharding import Mesh
from jax.sharding import PartitionSpec as P

HEADS = 8
Z_HI = 4
CORES = 2
Z_LO = 4
QUERY_BLOCK = 256
EPS = 1e-05
ROW_CHUNK = 16
COL = ("z_hi", "core", "x")
ROW = ("z_lo", "y")


def contract(a, b, dim_a, dim_b):
    dims = (((dim_a,), (dim_b,)), ((), ()))
    return lax.dot_general(a, b, dims, preferred_element_type=jnp.float32)


def layer_norm(values, gain):
    centred = values - jnp.mean(values, axis=-1, keepdims=True)
    variance = jnp.mean(centred * centred, axis=-1, keepdims=True)
    return (centred * lax.rsqrt(variance + EPS) * gain).astype(jnp.bfloat16)


def lines_kernel(*refs, lines, passed):
    (cells_ref, gain_ref, qkv_ref, out_ref), refs = refs[:4], refs[4:]
    sources, result_ref, targets = refs[:passed], refs[passed], refs[passed + 1 : 2 * passed + 1]
    q_ref, kt_ref, v_ref, att_ref, *sems = refs[2 * passed + 1 :]
    copies = [pltpu.make_async_copy(s, t, sems[0].at[n]) for n, (s, t) in enumerate(zip(sources, targets))]
    for copy in copies:
        copy.start()
    attend_lines(cells_ref, gain_ref, qkv_ref, out_ref, result_ref, q_ref, kt_ref, v_ref, att_ref, lines)
    for copy in copies:
        copy.wait()


def attend_lines(cells_ref, gain_ref, qkv_ref, out_ref, result_ref, q_ref, kt_ref, v_ref, att_ref, lines):
    cells, width = cells_ref.shape
    length = cells // lines
    head_dim = width // HEADS
    scale = head_dim**-0.5 * math.log2(math.e)
    normed = layer_norm(cells_ref[...].astype(jnp.float32), gain_ref[...])
    q_ref[...] = (contract(normed, qkv_ref[:, :width], 1, 0) * scale).astype(jnp.bfloat16)
    kt_ref[...] = contract(qkv_ref[:, width : 2 * width], normed, 0, 1).astype(jnp.bfloat16)
    v_ref[...] = contract(normed, qkv_ref[:, 2 * width :], 1, 0).astype(jnp.bfloat16)
    block = min(QUERY_BLOCK, length)
    head_of_v = lax.broadcasted_iota(jnp.int32, (length, width), 1) // head_dim
    head_of_q = lax.broadcasted_iota(jnp.int32, (block, width), 1) // head_dim
    zero, one = jnp.zeros((), jnp.bfloat16), jnp.ones((), jnp.bfloat16)
    for line in range(lines):
        keys = slice(line * length, (line + 1) * length)
        for start in range(line * length, (line + 1) * length, block):
            rows = slice(start, start + block)
            attended = jnp.zeros((block, width), jnp.float32)
            for head in range(HEADS):
                queries = jnp.where(head_of_q == head, q_ref[rows, :], zero)
                scores = contract(queries, kt_ref[:, keys], 1, 0)
                peak = jnp.max(scores, axis=1, keepdims=True)
                shares = jnp.exp2(scores - peak).astype(jnp.bfloat16)
                values = jnp.where(head_of_v == head, v_ref[keys, :], one)
                total = contract(shares, values, 1, 0)
                half = width // 2
                sums = jnp.concatenate([total[:, half:], total[:, :half]], axis=1)
                attended = jnp.where(head_of_q == head, total / sums, attended)
            att_ref[rows, :] = attended.astype(jnp.bfloat16)
    added = contract(att_ref[...], out_ref[...], 1, 0)
    result_ref[...] = (cells_ref[...].astype(jnp.float32) + added).astype(jnp.bfloat16)


def attend(cells, gain, qkv, out, lines, passed=()):
    count, width = cells.shape
    whole, anywhere = pl.BlockSpec(memory_space=pltpu.VMEM), pl.BlockSpec(memory_space=pl.ANY)
    results = pl.pallas_call(
        functools.partial(lines_kernel, lines=lines, passed=len(passed)),
        out_shape=[jax.ShapeDtypeStruct(a.shape, a.dtype) for a in (cells, *passed)],
        in_specs=[whole] * 4 + [anywhere] * len(passed),
        out_specs=[whole] * (1 + len(passed)),
        scratch_shapes=[
            pltpu.VMEM((count, width), jnp.bfloat16),
            pltpu.VMEM((width, count), jnp.bfloat16),
            pltpu.VMEM((count, width), jnp.bfloat16),
            pltpu.VMEM((count, width), jnp.bfloat16),
        ]
        + ([pltpu.SemaphoreType.DMA((len(passed),))] if passed else []),
        compiler_params=pltpu.CompilerParams(vmem_limit_bytes=40 << 20),
        name=f"attend_{lines}_lines",
    )(cells, gain, qkv, out, *passed)
    return results if passed else results[0]


def interleave_kernel(home_ref, grid_ref):
    places, pair, _, width = home_ref.shape
    rows = grid_ref.shape[0]
    start = pl.multiple_of(pl.program_id(0) * rows, rows)
    lines = home_ref[:, :, pl.ds(start, rows), :].reshape(places * pair, rows, width)
    grid_ref[...] = jnp.swapaxes(lines, 0, 1)


def interleave(home):
    places, pair, rows, width = home.shape
    return pl.pallas_call(
        interleave_kernel,
        out_shape=jax.ShapeDtypeStruct((rows, places * pair, width), home.dtype),
        grid=(rows // ROW_CHUNK,),
        in_specs=[pl.BlockSpec(memory_space=pltpu.VMEM)],
        out_specs=pl.BlockSpec((ROW_CHUNK, places * pair, width), lambda chunk: (chunk, 0, 0)),
        compiler_params=pltpu.CompilerParams(vmem_limit_bytes=16 << 20),
        name="interleave_columns",
    )(home)


def on_device(grid, row_gain, row_qkv, row_out, col_gain, col_qkv, col_out):
    rows_blk, cols_blk, width = grid.shape
    col_count = lax.axis_size(COL)
    row_count = lax.axis_size(ROW)
    pair = cols_blk // row_count
    cells = lax.all_to_all(grid, COL, split_axis=0, concat_axis=0, tiled=True)
    col_weights = (col_gain.reshape(1, width), col_qkv, col_out)
    middle, *col_weights = attend(
        cells.reshape(-1, width), row_gain.reshape(1, width), row_qkv, row_out, 1, col_weights
    )
    to_cols = middle.reshape(col_count * row_count, pair, width)
    col_cells = lax.all_to_all(to_cols, (*COL, *ROW), split_axis=0, concat_axis=0, tiled=True)
    lines = col_cells.transpose(1, 0, 2).reshape(-1, width)
    updated = attend(lines, *col_weights, pair)
    back = updated.reshape(pair, col_count, row_count, width).transpose(2, 0, 1, 3)
    home = lax.all_to_all(back, ROW, split_axis=0, concat_axis=0, tiled=True)
    return interleave(home)


def solution(mesh):
    row_count, _ = mesh.devices.shape
    split = Mesh(mesh.devices.reshape(row_count // Z_LO, Z_LO, Z_HI, -1, CORES), ("y", "z_lo", "z_hi", "x", "core"))
    in_specs = (P(("y", "z_lo"), ("z_hi", "x", "core"), None), P(), P(), P(), P(), P(), P())
    out_specs = P(("y", "z_lo"), ("z_hi", "x", "core"), None)
    return jax.shard_map(
        on_device, mesh=split, in_specs=in_specs, out_specs=out_specs, check_vma=False
    )
```
